32 devices in a mesh: gy: 8 (over y, x, core), gx: 4 (over z).
Axes of the slice: x: 2, y: 2, z: 4, core: 2. Of those that a mesh axis runs over, the one named last changes fastest.
Arguments:
- velocity: bfloat16 [3, 32, 1536, 1536], P(None, 'gy', 'gx'), may hold values from -40 to 40
- ref_planes: int32 [6], replicated, may hold values from 4 to 27, as said below
- partner_offsets: int32 [8], replicated, may hold values from -4 to 4, as said below
- band_owner: int32 [48], replicated, may hold values from 0 to 7, as said below
Outputs:
- correlations: float32 [96, 9, 384, 384], P('gy', None, 'gx')
The draws below stay inside these ranges and needn't reach their ends.
Inputs may be any that keep to these rules, and one draw needn't show every extreme that they name: `ref_planes`: 6 distinct planes; 4 and 27 are among them. `partner_offsets`: 8 distinct offsets; -4 and 4 are among them. `band_owner`: the pairs owned by one index of gy are consecutive; no index owns more than 12 pairs and one owns exactly 12.
All inputs are finite; a program needn't handle non-finite values.
Results may differ from the reference program's by a relative error of at most 0.0035.
Values may be sent and summed in bfloat16 or wider, within the bound.
A program may use at most 256 MiB of HBM per device.

```python
import math
import jax
import jax.numpy as jnp
from jax import lax

NX = 1536
NZ = 1536
NY = 32
NREF = 6
NOFF = 8
PAIRS = 48
SLOTS = 12
LX = 384
LZ = 384
N_GY = 8


def bridge_along(noise, axis, length):
    summed = jnp.cumsum(noise, axis=axis)
    last = jnp.take(summed, jnp.array([length - 1]), axis=axis)
    shape = [1] * noise.ndim
    shape[axis] = length
    ramp = ((jnp.arange(length, dtype=jnp.float32) + 1.0) / length).reshape(shape)
    return jnp.clip((summed - ramp * last) / math.sqrt(length) * 2.0, -6.0, 6.0)


def draw_velocity(key, part):
    key_noise = jax.random.fold_in(key, 11)
    key_fresh = jax.random.fold_in(key, 12)
    key_wave = jax.random.fold_in(key, 13)
    key_amp = jax.random.fold_in(key, 14)
    key_phase = jax.random.fold_in(key, 16)
    memory = 0.75
    renew = math.sqrt(1.0 - memory * memory)
    waves = jax.random.randint(key_wave, (NY,), 2, 10).astype(jnp.float32)
    phases = jax.random.uniform(key_phase, (NY,), jnp.float32, -math.pi, math.pi)
    span_pos = jnp.arange(NZ, dtype=jnp.float32)
    amplitude = jax.random.uniform(key_amp, (NY, 3, 1, 1), jnp.float32, 0.5, 1.5)

    def fresh(plane_index):
        plane_key = jax.random.fold_in(key_fresh, plane_index)
        streak = bridge_along(jax.random.normal(jax.random.fold_in(plane_key, 1), (3, NX, NZ), jnp.float32), 1, NX)
        spanwise = bridge_along(jax.random.normal(jax.random.fold_in(plane_key, 2), (3, NX, NZ), jnp.float32), 2, NZ)
        modulation = 1.0 + 0.8 * jnp.cos(2.0 * math.pi * waves[plane_index] * span_pos / NZ + phases[plane_index])
        return streak * modulation[None, None, :] + spanwise

    def plane_noise(plane_index):
        noise_key = jax.random.fold_in(key_noise, plane_index)
        return jax.random.truncated_normal(noise_key, -5.0, 5.0, (3, NX, NZ), jnp.float32)

    def advance(shared, plane_index):
        shared = jnp.where(plane_index == 0, fresh(plane_index), jnp.clip(memory * shared + renew * fresh(plane_index), -12.0, 12.0))
        field = plane_noise(plane_index) + amplitude[plane_index] * shared
        return (shared, field.astype(jnp.bfloat16))
    start = jnp.zeros((3, NX, NZ), jnp.float32)
    final, planes = lax.scan(advance, start, jnp.arange(NY, dtype=jnp.int32))
    return planes.transpose(1, 0, 2, 3)


def draw_ref_planes(key, part):
    key_pick = jax.random.fold_in(key, 21)
    key_order = jax.random.fold_in(key, 22)
    inner = jax.random.permutation(key_pick, NY - 10) + 5
    chosen = jnp.concatenate([jnp.array([4, NY - 5], dtype=jnp.int32), inner[:NREF - 2].astype(jnp.int32)])
    return jax.random.permutation(key_order, chosen).astype(jnp.int32)


def draw_partner_offsets(key, part):
    key_drop = jax.random.fold_in(key, 31)
    key_order = jax.random.fold_in(key, 32)
    dropped = jax.random.randint(key_drop, (), -3, 4)
    values = jnp.arange(8, dtype=jnp.int32) - 4
    values = values + (values >= dropped).astype(jnp.int32)
    return jax.random.permutation(key_order, values).astype(jnp.int32)


def draw_band_owner(key, part):
    key_caps = jax.random.fold_in(key, 41)
    key_order = jax.random.fold_in(key, 42)
    lowest = (SLOTS + 1) // 2
    capacity = jax.random.randint(key_caps, (N_GY,), lowest, SLOTS + 1)
    device_order = jax.random.permutation(key_order, N_GY).astype(jnp.int32)
    ordered_caps = capacity[device_order].at[0].set(SLOTS)
    band_ends = jnp.cumsum(ordered_caps)
    positions = jnp.arange(PAIRS, dtype=jnp.int32)
    position_band = jnp.sum((band_ends[None, :] <= positions[:, None]).astype(jnp.int32), axis=1)
    position_band = jnp.minimum(position_band, N_GY - 1)
    return device_order[position_band].astype(jnp.int32)


def setup_inputs(seed: int = 0) -> dict:
    splits = jax.random.split(jax.random.key(seed), 5)
    return {
        "velocity": draw_velocity(jax.random.fold_in(splits[4], 71), 0),
        "ref_planes": draw_ref_planes(jax.random.fold_in(splits[4], 71), 0),
        "partner_offsets": draw_partner_offsets(jax.random.fold_in(splits[4], 71), 0),
        "band_owner": draw_band_owner(jax.random.fold_in(splits[4], 71), 0),
    }


def angle_table(count_rows, count_cols, length):
    rows = jnp.arange(count_rows, dtype=jnp.int32)
    cols = jnp.arange(count_cols, dtype=jnp.int32)
    phase = (rows[:, None] * cols[None, :]) % length
    return (2.0 * math.pi / length) * phase.astype(jnp.float32)


def reference(velocity, ref_planes, partner_offsets, band_owner):
    half = NZ // 2
    z_angle = angle_table(NZ, half, NZ)
    forward_z = jnp.concatenate([jnp.cos(z_angle), -jnp.sin(z_angle)], axis=1).astype(jnp.bfloat16)
    x_angle = angle_table(NX, NX, NX)
    cos_x = jnp.cos(x_angle).astype(jnp.bfloat16)
    sin_x = jnp.sin(x_angle).astype(jnp.bfloat16)
    lag_angle_x = angle_table(LX, LX, LX)
    cos_lag = jnp.cos(lag_angle_x)
    sin_lag = jnp.sin(lag_angle_x)
    lag_angle_z = angle_table(LZ, LZ, LZ)
    cos_span = jnp.cos(lag_angle_z)
    sin_span = jnp.sin(lag_angle_z)
    norm_scale = 1.0 / float(NX * NZ) ** 2
    highest = lax.Precision.HIGHEST

    def spectrum(plane_index):
        plane = lax.dynamic_index_in_dim(velocity, plane_index, 1, keepdims=False)
        along_z = jnp.dot(plane.reshape(3 * NX, NZ), forward_z, preferred_element_type=jnp.float32).astype(jnp.bfloat16)
        columns = along_z.reshape(3, NX, NZ).transpose(1, 0, 2).reshape(NX, 3 * NZ)
        cosine_part = jnp.dot(cos_x, columns, preferred_element_type=jnp.float32).reshape(NX, 3, 2, half)
        sine_part = jnp.dot(sin_x, columns, preferred_element_type=jnp.float32).reshape(NX, 3, 2, half)
        real_part = cosine_part[:, :, 0] + sine_part[:, :, 1]
        imag_part = cosine_part[:, :, 1] - sine_part[:, :, 0]
        return jnp.stack([real_part, imag_part])

    spectra = lax.map(spectrum, jnp.arange(NY, dtype=jnp.int32))
    weight = jnp.where(jnp.arange(half, dtype=jnp.int32) == 0, 1.0, 2.0).astype(jnp.float32)

    def pair_lags(pair_index):
        ref_index = ref_planes[pair_index // NOFF]
        other_index = ref_index + partner_offsets[pair_index % NOFF]
        left = spectra[ref_index] * weight
        right = spectra[other_index]
        prod_real = left[0][:, :, None, :] * right[0][:, None, :, :] + left[1][:, :, None, :] * right[1][:, None, :, :]
        prod_imag = left[0][:, :, None, :] * right[1][:, None, :, :] - left[1][:, :, None, :] * right[0][:, None, :, :]
        fold_real = prod_real.reshape(4, LX, 3, 3, 2, LZ).sum(axis=(0, 4))
        fold_imag = prod_imag.reshape(4, LX, 3, 3, 2, LZ).sum(axis=(0, 4))
        lag_real = jnp.einsum('ka,kijz->ijaz', cos_lag, fold_real, precision=highest) - jnp.einsum('ka,kijz->ijaz', sin_lag, fold_imag, precision=highest)
        lag_imag = jnp.einsum('ka,kijz->ijaz', sin_lag, fold_real, precision=highest) + jnp.einsum('ka,kijz->ijaz', cos_lag, fold_imag, precision=highest)
        lagged = jnp.einsum('ijaz,zb->ijab', lag_real, cos_span, precision=highest) - jnp.einsum('ijaz,zb->ijab', lag_imag, sin_span, precision=highest)
        return (lagged * norm_scale).reshape(9, LX, LZ)

    results = lax.map(pair_lags, jnp.arange(PAIRS, dtype=jnp.int32))
    pair_order = jnp.arange(PAIRS, dtype=jnp.int32)
    same_owner = band_owner[:, None] == band_owner[None, :]
    earlier = pair_order[None, :] < pair_order[:, None]
    slot_of = jnp.sum((same_owner & earlier).astype(jnp.int32), axis=1).astype(jnp.int32)
    dest_row = (band_owner * SLOTS + slot_of).astype(jnp.int32)
    output = jnp.zeros((SLOTS * N_GY, 9, LX, LZ), jnp.float32)
    return output.at[dest_row].set(results)
```

```python
import functools
import math

import jax
import jax.numpy as jnp
import numpy as np
from jax import lax
from jax.experimental import pallas as pl
from jax.experimental.pallas import tpu as pltpu
from jax.sharding import PartitionSpec as P

LANES = 128
ROWS = 8


def circle(rows, cols, length):
    phase = np.asarray(rows, np.int64)[:, None] * np.asarray(cols, np.int64)[None, :] % length
    return 2.0 * np.pi / length * phase


def mode_members(lag_z, slots):
    half = lag_z // 2
    k = np.arange(slots)
    mirror = np.where(k == 0, half, lag_z - k)
    members = np.stack([k, k + lag_z, mirror, mirror + lag_z])
    return members, k < half


def forward_z_table(width_z, lag_z, devices, block_len):
    members, used = mode_members(lag_z, devices * block_len)
    angle = circle(members.reshape(-1), np.arange(width_z), width_z)
    sign = np.repeat(np.array([-1.0, -1.0, 1.0, 1.0]), devices * block_len)[:, None]
    table = np.stack([np.cos(angle), sign * np.sin(angle)])
    table = table.reshape(2, 4, devices * block_len, width_z) * used[None, None, :, None]
    table = table.reshape(2, 4, devices, block_len, width_z).transpose(2, 0, 1, 3, 4)
    return table.reshape(-1, width_z).astype(np.float32).astype(jnp.bfloat16)


def span_table(lag_z, devices, block_len):
    slots = devices * block_len
    k = np.arange(slots)
    t = np.arange(lag_z)
    angle = circle(k, t, lag_z)
    real = np.cos(angle)
    imag = -np.sin(angle)
    imag[0] = np.cos(np.pi * t)
    table = np.stack([real, imag]) * (k < lag_z // 2)[None, :, None]
    table = table.reshape(2, devices, block_len, lag_z).transpose(2, 0, 1, 3)
    return table.reshape(-1, lag_z).astype(np.float32).astype(jnp.bfloat16)


def fold_kernel(
    comps, planes_dev, block_len, row_count, col_count, off_count,
    refs, offs, got, cos_ref, sin_ref, weight_ref, out, spec, lhs,
):
    part_rows = 4 * block_len
    group = 2 * part_rows
    x_dev = got.shape[2] // (comps * planes_dev)
    pairs = out.shape[1]
    spec[...] = jnp.zeros_like(spec)

    def transform(g, carry):
        for n in range(comps * planes_dev):
            for col in range(col_count):
                lhs[n * group : (n + 1) * group, col * x_dev : (col + 1) * x_dev] = got[
                    g * col_count + col, :, n * x_dev : (n + 1) * x_dev
                ]
        cosine = jnp.dot(lhs[...], cos_ref[...], preferred_element_type=jnp.float32)
        sine = jnp.dot(lhs[...], sin_ref[...], preferred_element_type=jnp.float32)
        for n in range(comps * planes_dev):
            comp, plane = n // planes_dev, n % planes_dev
            y = g * planes_dev + plane
            a = n * group
            b = a + part_rows
            parts = (
                cosine[a:b] + sine[b : b + part_rows],
                cosine[b : b + part_rows] - sine[a:b],
            )
            for ri in range(2):
                weighted = parts[ri] * weight_ref[...]
                for mem in range(4):
                    lo = mem * block_len
                    spec[ri, mem, y, comp, 0:block_len, :] = weighted[lo : lo + block_len]
                for mem in range(2):
                    lo = (mem + 2) * block_len
                    spec[ri, mem, y, comp, block_len : block_len + 1, :] = parts[ri][lo : lo + 1]
        return carry

    lax.fori_loop(0, row_count, transform, 0)

    def fold(pair, carry):
        left = refs[pair // off_count]
        right = left + offs[pair % off_count]
        real = [None] * (comps * comps)
        imag = [None] * (comps * comps)
        for mem in range(4):
            for m in range(4):
                lanes = slice(m * LANES, (m + 1) * LANES)
                lr = [spec[0, mem, left, c, :, lanes] for c in range(comps)]
                li = [spec[1, mem, left, c, :, lanes] for c in range(comps)]
                rr = [spec[0, mem, right, c, :, lanes] for c in range(comps)]
                rim = [spec[1, mem, right, c, :, lanes] for c in range(comps)]
                for i in range(comps):
                    for j in range(comps):
                        n = i * comps + j
                        re = lr[i] * rr[j] + li[i] * rim[j]
                        im = lr[i] * rim[j] - li[i] * rr[j]
                        real[n] = re if real[n] is None else real[n] + re
                        imag[n] = im if imag[n] is None else imag[n] + im
        for n in range(comps * comps):
            out[0, pair, n] = real[n]
            out[1, pair, n] = imag[n]
        return carry

    lax.fori_loop(0, pairs, fold, 0)


def spread_kernel(block_count, scale, count, got, table, out):
    width = got.shape[2] // block_count
    live = pl.program_id(0) < count[0]
    for n in range(got.shape[0]):
        block = got[n]
        stacked = jnp.concatenate(
            [block[:, i * width : (i + 1) * width] for i in range(block_count)], axis=0
        )
        lagged = lax.dot_general(
            stacked, table[...], (((0,), (0,)), ((), ())), preferred_element_type=jnp.float32
        )
        out[0, n] = jnp.where(live, lagged * scale, 0.0)


def per_device(velocity, ref_planes, partner_offsets, band_owner):
    row_count = lax.axis_size("gy")
    col_count = lax.axis_size("gx")
    devices = row_count * col_count
    comps, planes_dev, x_dev, width_z = velocity.shape
    width_x = x_dev * col_count
    lag_z = width_z // 4
    lag_x = width_x // 4
    lag_block = lag_x // col_count
    block_len = (lag_z // 2 + devices - 1) // devices
    row_id = lax.axis_index("gy")
    device_id = row_id * col_count + lax.axis_index("gx")
    first = device_id == 0
    norm_scale = 2.0 / float(width_x * width_z) ** 2
    refs = ref_planes.shape[0]
    offs = partner_offsets.shape[0]
    pairs = refs * offs
    squares = comps * comps
    planes = planes_dev * row_count

    table_z = jnp.asarray(forward_z_table(width_z, lag_z, devices, block_len))
    along_z = lax.dot_general(
        table_z,
        velocity.reshape(comps * planes_dev * x_dev, width_z),
        (((1,), (1,)), ((), ())),
        preferred_element_type=jnp.float32,
    ).astype(jnp.bfloat16)
    parcels = along_z.reshape(devices, 8 * block_len, comps * planes_dev * x_dev)
    got = lax.all_to_all(parcels, ("gy", "gx"), split_axis=0, concat_axis=0, tiled=True)

    tiles = lag_x // LANES
    angle_x = circle(np.arange(width_x), np.arange(width_x), width_x)
    angle_x = angle_x.reshape(width_x, 4, tiles, LANES).transpose(0, 2, 1, 3)
    angle_x = angle_x.reshape(width_x, width_x)
    cos_x = jnp.asarray(np.cos(angle_x).astype(np.float32).astype(jnp.bfloat16))
    sin_x = jnp.asarray(np.sin(angle_x).astype(np.float32).astype(jnp.bfloat16))

    plain = np.ones((4, block_len), np.float32)
    zero_mode = plain.copy()
    zero_mode[0, 0] = math.sqrt(0.5)
    zero_mode[2:, 0] = 0.0
    weight = jnp.where(first, zero_mode.reshape(-1), plain.reshape(-1))
    weight = jnp.broadcast_to(weight[:, None], (4 * block_len, 4 * LANES))

    lines = comps * planes_dev * 8 * block_len
    folded = pl.pallas_call(
        functools.partial(
            fold_kernel, comps, planes_dev, block_len, row_count, col_count, offs
        ),
        grid_spec=pltpu.PrefetchScalarGridSpec(
            num_scalar_prefetch=2,
            grid=(tiles,),
            in_specs=[
                pl.BlockSpec(got.shape, lambda t, *_: (0, 0, 0), pipeline_mode=pl.Buffered(1)),
                pl.BlockSpec((width_x, 4 * LANES), lambda t, *_: (0, t)),
                pl.BlockSpec((width_x, 4 * LANES), lambda t, *_: (0, t)),
                pl.BlockSpec((4 * block_len, 4 * LANES), lambda t, *_: (0, 0)),
            ],
            out_specs=pl.BlockSpec(
                (2, pairs, squares, ROWS, LANES), lambda t, *_: (0, 0, 0, 0, t)
            ),
            scratch_shapes=[
                pltpu.VMEM((2, 4, planes, comps, ROWS, 4 * LANES), jnp.float32),
                pltpu.VMEM((lines, width_x), jnp.bfloat16),
            ],
        ),
        out_shape=jax.ShapeDtypeStruct((2, pairs, squares, ROWS, lag_x), jnp.float32),
        compiler_params=pltpu.CompilerParams(vmem_limit_bytes=58 * 2**20),
        name="transform_and_fold",
    )(ref_planes, partner_offsets, got, cos_x, sin_x, weight)

    angle_lag = circle(np.arange(lag_x), np.arange(lag_x), lag_x).reshape(
        lag_x, col_count, 1, lag_block
    )
    from_real = np.concatenate([np.cos(angle_lag), np.sin(angle_lag)], axis=2)
    from_imag = np.concatenate([-np.sin(angle_lag), np.cos(angle_lag)], axis=2)
    from_real = from_real.reshape(lag_x, 2 * lag_x).astype(np.float32)
    from_imag = from_imag.reshape(lag_x, 2 * lag_x).astype(np.float32)
    flat = folded.reshape(2, pairs * squares * ROWS, lag_x)
    lags = jnp.dot(flat[0], from_real, precision=lax.Precision.HIGH) + jnp.dot(
        flat[1], from_imag, precision=lax.Precision.HIGH
    )
    lags = lags.astype(jnp.bfloat16).reshape(pairs, squares, ROWS, col_count, 2, lag_block)
    zero_imag = jnp.where(first, lags[:, :, block_len, :, 0], lags[:, :, 0, :, 1])
    slot_ids = jnp.arange(ROWS, dtype=jnp.int32)[None, None, :, None, None, None]
    part_ids = jnp.arange(2, dtype=jnp.int32)[None, None, None, None, :, None]
    lags = jnp.where(
        (slot_ids == 0) & (part_ids == 1), zero_imag[:, :, None, :, None, :], lags
    )[:, :, :block_len]

    slot_count = (2 * pairs + row_count - 1) // row_count
    owners = jnp.arange(row_count, dtype=jnp.int32)
    owned = band_owner[None, :] == owners[:, None]
    counts = jnp.sum(owned.astype(jnp.int32), axis=1)
    order = jnp.arange(pairs, dtype=jnp.int32)
    starts = jnp.min(jnp.where(owned, order[None, :], pairs - 1), axis=1)
    source = starts[:, None] + jnp.arange(slot_count, dtype=jnp.int32)[None, :]
    source = jnp.minimum(source, pairs - 1).reshape(-1)
    ready = lags.transpose(0, 3, 1, 2, 4, 5).reshape(
        pairs, col_count, squares, block_len * 2 * lag_block
    )
    placed = jnp.take(ready, source, axis=0, mode="clip")
    placed = placed.reshape(row_count, slot_count, col_count, squares, -1)
    placed = placed.transpose(0, 2, 1, 3, 4).reshape(devices, slot_count * squares, -1)
    arrived = lax.all_to_all(placed, ("gy", "gx"), split_axis=0, concat_axis=0, tiled=True)
    arrived = arrived.transpose(1, 0, 2)

    table_span = jnp.asarray(span_table(lag_z, devices, block_len))
    own_count = lax.dynamic_slice_in_dim(counts, row_id, 1)
    return pl.pallas_call(
        functools.partial(spread_kernel, 2 * block_len, norm_scale),
        grid_spec=pltpu.PrefetchScalarGridSpec(
            num_scalar_prefetch=1,
            grid=(slot_count,),
            in_specs=[
                pl.BlockSpec((squares, devices, arrived.shape[2]), lambda s, *_: (s, 0, 0)),
                pl.BlockSpec(table_span.shape, lambda s, *_: (0, 0)),
            ],
            out_specs=pl.BlockSpec((1, squares, lag_block, lag_z), lambda s, *_: (s, 0, 0, 0)),
        ),
        out_shape=jax.ShapeDtypeStruct((slot_count, squares, lag_block, lag_z), jnp.float32),
        compiler_params=pltpu.CompilerParams(vmem_limit_bytes=32 * 2**20),
        name="span_lags",
    )(own_count, arrived, table_span)


def solution(mesh):
    placed = (P(None, "gy", "gx", None), P(), P(), P())
    return jax.shard_map(
        per_device, mesh=mesh, in_specs=placed, out_specs=P("gy", None, "gx", None), check_vma=False
    )
```
